256 devices in a mesh: blk: 32 (over y, z), img: 4 (over x_lo, core), doc: 2 (over x_hi).
Axes of the slice: x: 4 (x_hi: 2, x_lo: 2; x = x_hi * 2 + x_lo), y: 4, z: 8, core: 2. Of those that a mesh axis runs over, the one named last changes fastest.
Arguments:
- features: bfloat16 [64, 257, 1280], P(('doc', 'blk')), parts along dimension 0, may hold values from -6 to 6
- latents: bfloat16 [64, 1280], replicated, may hold values from -6 to 6
- context_gain: float32 [1280], replicated, may hold values from 0.25 to 1.75
- latent_gain: float32 [1280], replicated, may hold values from 0.25 to 1.75
- final_gain: float32 [1280], replicated, may hold values from 0.25 to 1.75
- rs_query: bfloat16 [1280, 1536], P('blk', 'img'), may hold values from -0.15625 to 0.15625
- rs_key: bfloat16 [1280, 1536], P('blk', 'img'), may hold values from -0.15625 to 0.15625
- rs_value: bfloat16 [1280, 1536], P('blk', 'img'), may hold values from -0.15625 to 0.15625
- rs_out: bfloat16 [1536, 1280], P('img', 'blk'), may hold values from -0.15625 to 0.15625
- x_key: bfloat16 [1280, 4096], P(None, 'img'), may hold values from -0.15625 to 0.15625
- x_value: bfloat16 [1280, 4096], P(None, 'img'), may hold values from -0.15625 to 0.15625
- text_query: bfloat16 [8192, 4096], P(('doc', 'blk'), 'img'), parts along dimension 0, may hold values from -180 to 180
- text_key: bfloat16 [8192, 4096], P(('doc', 'blk'), 'img'), parts along dimension 0, may hold values from -6 to 6
- text_value: bfloat16 [8192, 4096], P(('doc', 'blk'), 'img'), parts along dimension 0, may hold values from -6 to 6
- cross_query: bfloat16 [8192, 4096], P(('doc', 'blk'), 'img'), parts along dimension 0, may hold values from -240 to 240
- cross_gate: float32 [4096], P('img'), may hold values from -1.5 to 1.5
- image_pos: int32 [64], P('doc'), parts along dimension 0, may hold values from 0 to 4095, as said below
Outputs:
- cross_out: bfloat16 [8192, 4096], P(('doc', 'blk'), 'img'), parts along dimension 0
- self_out: bfloat16 [8192, 4096], P(('doc', 'blk'), 'img'), parts along dimension 0
The draws below stay inside these ranges and needn't reach their ends.
There are 2 independent parts, one for each index of `doc`. The reference program is written for one: setup_inputs(seed, part) draws one part's arguments, and reference() takes and returns one part's arrays. A program takes and returns all parts, laid end to end along the dimension named above; an argument that names none is the same for every part. Nothing has to cross between parts.
Inputs may be any that keep to these rules, and one draw needn't show every extreme that they name: `image_pos`: all different, in no particular order; the 128 positions of one blk index hold at most 3 of them, and some blk index holds exactly 3; one image stands at the last position.
All inputs are finite; a program needn't handle non-finite values.
Results may differ from the reference program's by a relative error of at most 0.04.
Values may be sent and summed in bfloat16 or wider, within the bound.
No kernel may reach another device: no remote copies, remote signals or barrier semaphores. Data moves between devices by JAX's collectives and lax.ppermute only.
A program may use at most 128 MiB of HBM per device.

```python
import jax
import jax.numpy as jnp
from jax import lax

HEADS = 32
HD = 128
VIS = 1280
LAT = 64
RHEADS = 16
RHD = 96
PATCH = 257
TOK_DEV = 128
CITE = 3
TOKENS = 4096
IMAGES = 32


def shared_keys(key):
    return jnp.clip(jax.random.normal(key, (TOKENS, HEADS * HD), jnp.float32), -6.0, 6.0)


def draw_text_key(key, part):
    base_rows = shared_keys(key)
    return base_rows.astype(jnp.bfloat16)


def draw_text_query(key, part):
    key = jax.random.fold_in(key, 7)
    first_key = jax.random.fold_in(key, 0)
    array_shape = (TOKENS, HEADS * HD)
    drawn_values = jnp.clip(jax.random.normal(first_key, array_shape, jnp.float32), -6.0, 6.0)
    return drawn_values.astype(jnp.bfloat16)


def draw_cross_query(key, part):
    key = jax.random.fold_in(key, 9)
    first_key = jax.random.fold_in(key, 0)
    array_shape = (TOKENS, HEADS * HD)
    drawn_values = jnp.clip(jax.random.normal(first_key, array_shape, jnp.float32), -6.0, 6.0)
    return drawn_values.astype(jnp.bfloat16)


def draw_image_pos(key, part):
    key = jax.random.fold_in(key, 11)
    first_key, second_key, third_key, fourth_key = jax.random.split(key, 4)
    shard_count = TOKENS // TOK_DEV
    slot_count = shard_count * CITE
    full_shard = jax.random.randint(first_key, (), 0, shard_count)
    order = jax.random.permutation(second_key, slot_count)
    priority = (order // CITE == full_shard).astype(jnp.int32) + (order == slot_count - 1).astype(jnp.int32)
    ranking = jnp.argsort(-priority, stable=True)
    picked = jnp.sort(order[ranking][:IMAGES])
    spacing = TOK_DEV // CITE
    jitter = jax.random.randint(third_key, (IMAGES,), 0, spacing)
    jitter = jnp.where(picked == slot_count - 1, TOK_DEV - 1 - (CITE - 1) * spacing, jitter)
    sorted_pos = (picked // CITE * TOK_DEV + picked % CITE * spacing + jitter).astype(jnp.int32)
    assign = jax.random.permutation(fourth_key, IMAGES).astype(jnp.int32)
    first_rank = jnp.sum((picked // CITE < full_shard).astype(jnp.int32))
    target = ((full_shard + shard_count // 2) % shard_count).astype(jnp.int32)
    ranks = jnp.arange(IMAGES, dtype=jnp.int32)
    holder = jnp.sum(jnp.where(assign == target, ranks, 0))
    old_value = assign[first_rank]
    assign = jnp.where(ranks == first_rank, target, jnp.where(ranks == holder, old_value, assign))
    return jnp.zeros((IMAGES,), jnp.int32).at[assign].set(sorted_pos)


def levels(stream_key, extent, cuts, least, top_value):
    factor_of, own = 1.0, jax.random.fold_in(stream_key, 6)
    for axis_at, parts in cuts:
        heights = jnp.exp(jax.random.uniform(jax.random.fold_in(own, axis_at), (parts,), jnp.float32, least / len(cuts), top_value / len(cuts)))
        factor_of = factor_of * jnp.repeat(heights, extent[axis_at] // parts).reshape([-1 if axis == axis_at else 1 for axis in range(len(extent))])
    return factor_of


def noise(key, extent, deviation, reach, cuts=(), kind=jnp.bfloat16):
    level = levels(key, extent, cuts, -0.22, 0.18) if cuts else 1.0
    drawn = jax.random.normal(key, extent, jnp.float32) * deviation * level
    return jnp.minimum(jnp.maximum(drawn, -reach), reach).astype(kind)


def setup_inputs(seed: int = 0, part: int = 0) -> dict:
    keys = jax.random.split(jax.random.key(seed), 18)
    part_keys = jax.random.split(jax.random.fold_in(keys[17], part), 18)
    features = noise(part_keys[0], (IMAGES, PATCH, VIS), 1.0, 6.0, ((0, 32),))
    latents = noise(keys[1], (LAT, VIS), 1.0, 6.0)
    context_gain = jnp.clip(1.0 + 0.15 * jax.random.normal(keys[2], (VIS,), jnp.float32), 0.25, 1.75)
    latent_gain = jnp.clip(1.0 + 0.15 * jax.random.normal(keys[3], (VIS,), jnp.float32), 0.25, 1.75)
    final_gain = jnp.clip(1.0 + 0.15 * jax.random.normal(keys[4], (VIS,), jnp.float32), 0.25, 1.75)
    rs_query = noise(keys[5], (VIS, RHEADS * RHD), VIS ** -0.5, 0.15625, ((0, 32), (1, 4)))
    rs_key = noise(keys[6], (VIS, RHEADS * RHD), VIS ** -0.5, 0.15625, ((0, 32), (1, 4)))
    rs_value = noise(keys[7], (VIS, RHEADS * RHD), VIS ** -0.5, 0.15625, ((0, 32), (1, 4)))
    rs_out = noise(keys[8], (RHEADS * RHD, VIS), (RHEADS * RHD) ** -0.5, 0.15625, ((0, 4), (1, 32)))
    x_key = noise(keys[9], (VIS, HEADS * HD), VIS ** -0.5, 0.15625, ((1, 4),))
    x_value = noise(keys[10], (VIS, HEADS * HD), VIS ** -0.5, 0.15625, ((1, 4),))
    text_query = draw_text_query(jax.random.fold_in(jax.random.fold_in(keys[17], part), 71), part)
    text_key = draw_text_key(jax.random.fold_in(jax.random.fold_in(keys[17], part), 71), part)
    text_value = noise(part_keys[13], (TOKENS, HEADS * HD), 1.0, 6.0, ((0, 32), (1, 4)))
    cross_query = draw_cross_query(jax.random.fold_in(jax.random.fold_in(keys[17], part), 71), part)
    cross_gate = jnp.clip(jax.random.uniform(keys[15], (HEADS * HD,), jnp.float32, -1.5, 1.5) * levels(keys[15], (HEADS * HD,), ((0, 4),), -0.4, 0.0), -1.5, 1.5)
    image_pos = draw_image_pos(jax.random.fold_in(jax.random.fold_in(keys[17], part), 71), part)
    return dict(features=features, latents=latents, context_gain=context_gain, latent_gain=latent_gain, final_gain=final_gain, rs_query=rs_query, rs_key=rs_key, rs_value=rs_value, rs_out=rs_out, x_key=x_key, x_value=x_value, text_query=text_query, text_key=text_key, text_value=text_value, cross_query=cross_query, cross_gate=cross_gate, image_pos=image_pos)


epsilon = 1e-05

def layer_norm(values, gain):
    values = values.astype(jnp.float32)
    center = lax.optimization_barrier(jnp.mean(values, -1, keepdims=True))
    spread = lax.optimization_barrier(jnp.mean(jnp.square(values - center), -1, keepdims=True))
    return (values - center) * lax.rsqrt(spread + epsilon) * gain

def head_attention(query_rows, key_rows, value_rows, visible, head_width):
    scores = jnp.dot(query_rows, key_rows.T, preferred_element_type=jnp.float32) * head_width ** (-0.5)
    scores = jnp.where(visible, scores, -1e+30)
    row_peak = lax.optimization_barrier(jnp.max(scores, -1, keepdims=True))
    weights = jnp.where(visible, jnp.exp(scores - row_peak), 0.0)
    row_total = lax.optimization_barrier(jnp.sum(weights, -1, keepdims=True))
    return jnp.dot(weights.astype(jnp.bfloat16), value_rows, preferred_element_type=jnp.float32) / row_total

def resample(features, latents, context_gain, latent_gain, final_gain, rs_query, rs_key, rs_value, rs_out):
    latent_norm = layer_norm(latents, latent_gain).astype(jnp.bfloat16)
    query_all = jnp.dot(latent_norm, rs_query, preferred_element_type=jnp.float32).astype(jnp.bfloat16)

    def one_image(patches):
        feature_norm = layer_norm(patches, context_gain).astype(jnp.bfloat16)
        context = jnp.concatenate([feature_norm, latent_norm], 0)
        key_all = jnp.dot(context, rs_key, preferred_element_type=jnp.float32).astype(jnp.bfloat16)
        value_all = jnp.dot(context, rs_value, preferred_element_type=jnp.float32).astype(jnp.bfloat16)

        def one_head(head_index):

            def columns(matrix):
                return lax.dynamic_slice_in_dim(matrix, head_index * RHD, RHD, 1)
            return head_attention(columns(query_all), columns(key_all), columns(value_all), True, RHD)
        per_head = lax.map(one_head, jnp.arange(RHEADS, dtype=jnp.int32))
        head_context = jnp.transpose(per_head, (1, 0, 2)).reshape(LAT, RHEADS * RHD).astype(jnp.bfloat16)
        updated = latents.astype(jnp.float32) + jnp.dot(head_context, rs_out, preferred_element_type=jnp.float32)
        return layer_norm(updated, final_gain).astype(jnp.bfloat16)
    return lax.map(one_image, features)

def reference(features, latents, context_gain, latent_gain, final_gain, rs_query, rs_key, rs_value, rs_out, x_key, x_value, text_query, text_key, text_value, cross_query, cross_gate, image_pos):
    resampled = resample(features, latents, context_gain, latent_gain, final_gain, rs_query, rs_key, rs_value, rs_out)
    flat_latents = resampled.reshape(IMAGES * LAT, VIS)
    cross_keys = jnp.dot(flat_latents, x_key, preferred_element_type=jnp.float32).astype(jnp.bfloat16)
    cross_values = jnp.dot(flat_latents, x_value, preferred_element_type=jnp.float32).astype(jnp.bfloat16)
    positions = jnp.arange(TOKENS, dtype=jnp.int32)
    image_ids = jnp.arange(IMAGES, dtype=jnp.int32)
    reached = image_pos[None, :] <= positions[:, None]
    latest = lax.optimization_barrier(jnp.max(jnp.where(reached, image_pos[None, :], -1), axis=1))
    chosen = lax.optimization_barrier(jnp.sum(jnp.where(image_pos[None, :] == latest[:, None], image_ids[None, :], 0), axis=1))
    image_index = jnp.where(latest >= 0, chosen, -1).astype(jnp.int32)
    key_image = jnp.arange(IMAGES * LAT, dtype=jnp.int32) // LAT
    cross_visible = (key_image[None, :] == image_index[:, None]) | (image_index[:, None] < 0)
    causal = positions[None, :] <= positions[:, None]

    def text_head(head_index):

        def columns(matrix):
            return lax.dynamic_slice_in_dim(matrix, head_index * HD, HD, 1)
        cross_part = head_attention(columns(cross_query), columns(cross_keys), columns(cross_values), cross_visible, HD)
        self_part = head_attention(columns(text_query), columns(text_key), columns(text_value), causal, HD)
        return (cross_part, self_part)
    cross_heads, self_heads = lax.map(text_head, jnp.arange(HEADS, dtype=jnp.int32))
    cross_context = jnp.transpose(cross_heads, (1, 0, 2)).reshape(TOKENS, HEADS * HD)
    cross_out = jnp.where(image_index[:, None] >= 0, jnp.tanh(cross_gate) * cross_context, 0.0).astype(jnp.bfloat16)
    self_out = jnp.transpose(self_heads, (1, 0, 2)).reshape(TOKENS, HEADS * HD).astype(jnp.bfloat16)
    return (cross_out, self_out)
```

```python
import functools

import jax
import jax.numpy as jnp
from jax import lax
from jax.experimental import pallas as pl
from jax.experimental.pallas import tpu as pltpu
from jax.sharding import Mesh
from jax.sharding import PartitionSpec as P

HD = 128
RHD = 96
CITE = 3
BLK = ("y", "z")
IMG = ("xl", "core")
LOG2E = 1.4426950408889634

epsilon = 1e-05


def layer_norm(values, gain):
    values = values.astype(jnp.float32)
    center = jnp.mean(values, -1, keepdims=True)
    spread = jnp.mean(jnp.square(values - center), -1, keepdims=True)
    return (values - center) * lax.rsqrt(spread + epsilon) * gain


def attend(scores, visible, value_rows):
    scores = jnp.where(visible, scores, -1e30)
    row_peak = jnp.max(scores, -1, keepdims=True)
    weights = jnp.where(visible, jnp.exp(scores - row_peak), 0.0)
    row_total = jnp.sum(weights, -1)
    context = jnp.einsum(
        "hqk,khd->qhd", weights.astype(jnp.bfloat16), value_rows, preferred_element_type=jnp.float32
    )
    return context / jnp.transpose(row_total)[:, :, None]


def self_kernel(own_ref, q_ref, kv_ref, o_ref, s_ref):
    own = own_ref[0]
    pieces, blocks, rows2, width = kv_ref.shape
    rows = rows2 // 2
    group = 128 // rows
    factor = width**-0.5 * LOG2E
    index_q = lax.broadcasted_iota(jnp.int32, (128, 128), 0)
    index_k = lax.broadcasted_iota(jnp.int32, (128, 128), 1)
    place_q = index_q // rows * 128 + own * rows + index_q % rows
    place_k = index_k // rows * 128 + index_k % rows
    for turn in range(blocks // group):
        first = turn * group
        query = q_ref[first : first + group].reshape(128, width)
        span = (first + group) * rows
        peak = None
        for piece in range(pieces):
            keys = kv_ref[piece, 0 : first + group, 0:rows, :].reshape(span, width)
            scores = lax.dot_general(
                query, keys, (((1,), (1,)), ((), ())), preferred_element_type=jnp.float32
            )
            scores = scores * factor
            tail = jnp.where(place_k + piece * rows <= place_q, scores[:, span - 128 :], -1e30)
            s_ref[piece, :, span - 128 : span] = tail
            top = jnp.max(tail, -1, keepdims=True)
            if span > 128:
                s_ref[piece, :, 0 : span - 128] = scores[:, : span - 128]
                top = jnp.maximum(top, jnp.max(scores[:, : span - 128], -1, keepdims=True))
            peak = top if peak is None else jnp.maximum(peak, top)
        total = jnp.zeros((128, 1), jnp.float32)
        context = jnp.zeros((128, width), jnp.float32)
        for piece in range(pieces):
            weights = jnp.exp2(s_ref[piece, :, 0:span] - peak)
            total = total + jnp.sum(weights, -1, keepdims=True)
            values = kv_ref[piece, 0 : first + group, rows : 2 * rows, :].reshape(span, width)
            context = context + jnp.dot(
                weights.astype(jnp.bfloat16), values, preferred_element_type=jnp.float32
            )
        o_ref[first : first + group] = (
            (context / total).astype(jnp.bfloat16).reshape(group, rows, width)
        )


def self_attention(own, query, pairs):
    pieces, blocks, rows2, width = pairs.shape
    vmem = pl.BlockSpec(memory_space=pltpu.VMEM)
    return pl.pallas_call(
        self_kernel,
        out_shape=jax.ShapeDtypeStruct((blocks, rows2 // 2, width), jnp.bfloat16),
        in_specs=[pl.BlockSpec(memory_space=pltpu.SMEM), vmem, vmem],
        out_specs=vmem,
        scratch_shapes=[pltpu.VMEM((pieces, 128, blocks * rows2 // 2), jnp.float32)],
        compiler_params=pltpu.CompilerParams(vmem_limit_bytes=32 * 1024 * 1024),
        cost_estimate=pl.CostEstimate(
            flops=1200000000, bytes_accessed=3000000, transcendentals=2400000
        ),
        name="self_attention",
    )(own, query, pairs)


def by_head(rows, y_size, z_size):
    tokens = rows.shape[0]
    split = rows.reshape(y_size, tokens // y_size, z_size, HD)
    return jnp.transpose(split, (0, 2, 1, 3)).reshape(y_size * z_size, tokens // y_size, HD)


def shards(
    features,
    latents,
    context_gain,
    latent_gain,
    final_gain,
    rs_query,
    rs_key,
    rs_value,
    rs_out,
    x_key,
    x_value,
    text_query,
    text_key,
    text_value,
    cross_query,
    cross_gate,
    image_pos,
):
    y_size, z_size = lax.axis_size("y"), lax.axis_size("z")
    blocks = y_size * z_size
    heads_of = lax.axis_size(IMG)
    shard_index = lax.axis_index(BLK)
    own_y = lax.axis_index("y")
    tokens = text_query.shape[0]
    local_heads = text_query.shape[1] // HD
    piece = tokens // y_size
    latent_rows, full_width = latents.shape

    packed = jnp.concatenate(
        [by_head(part, y_size, z_size) for part in (text_query, text_key, text_value)], 1
    )
    packed = lax.all_to_all(packed, BLK, 0, 0, tiled=True)
    head_query = packed[:, 0:piece]
    pairs = lax.all_gather(packed[:, piece:], "y", axis=0, tiled=False)

    columns = rs_query.shape[1]
    bundle = jnp.concatenate([rs_query, rs_key, rs_value, jnp.transpose(rs_out)], 1)
    bundle = lax.all_gather(bundle, BLK, axis=0, tiled=True)
    latent_norm = layer_norm(latents, latent_gain).astype(jnp.bfloat16)
    feature_norm = layer_norm(features[0], context_gain).astype(jnp.bfloat16)
    context = jnp.concatenate([feature_norm, latent_norm], 0)
    query_rows = jnp.dot(latent_norm, bundle[:, :columns], preferred_element_type=jnp.float32)
    pair_rows = jnp.dot(
        context, bundle[:, columns : 3 * columns], preferred_element_type=jnp.float32
    )
    head_count = columns // RHD
    query_rows = query_rows.astype(jnp.bfloat16).reshape(latent_rows, head_count, RHD)
    pair_rows = pair_rows.astype(jnp.bfloat16)
    key_rows = pair_rows[:, :columns].reshape(-1, head_count, RHD)
    value_rows = pair_rows[:, columns:].reshape(-1, head_count, RHD)
    scores = jnp.einsum(
        "qhd,khd->hqk", query_rows, key_rows, preferred_element_type=jnp.float32
    ) * RHD ** (-0.5)
    head_context = (
        attend(scores, True, value_rows).astype(jnp.bfloat16).reshape(latent_rows, columns)
    )
    partial_out = lax.dot_general(
        head_context,
        bundle[:, 3 * columns :],
        (((1,), (1,)), ((), ())),
        preferred_element_type=jnp.float32,
    )
    quarter = latent_rows // heads_of
    summed = lax.psum_scatter(partial_out, IMG, scatter_dimension=0, tiled=True)
    own_latents = lax.dynamic_slice_in_dim(latents, lax.axis_index(IMG) * quarter, quarter, 0)
    resampled = layer_norm(own_latents.astype(jnp.float32) + summed, final_gain)
    resampled = resampled.astype(jnp.bfloat16)

    starts = jnp.arange(blocks, dtype=jnp.int32) * tokens
    image_rank = jnp.sum((image_pos[None, :] < image_pos[:, None]).astype(jnp.int32), axis=1)
    first_all = jnp.sum((image_pos[None, :] < starts[:, None]).astype(jnp.int32), axis=1)
    wanted = first_all[:, None] - 1 + jnp.arange(CITE + 1, dtype=jnp.int32)
    choice = (image_rank[None, None, :] == wanted[:, :, None]).astype(jnp.bfloat16)

    slots = CITE + 1
    spread = resampled.reshape(blocks, -1)
    spread = lax.all_to_all(spread, BLK, 0, 0, tiled=True)
    chosen = jnp.dot(
        choice.reshape(blocks * slots, -1), spread, preferred_element_type=jnp.float32
    ).astype(jnp.bfloat16)
    chosen = lax.all_to_all(chosen.reshape(blocks, slots, -1), BLK, 0, 0, tiled=True)
    chosen = chosen.reshape(quarter, blocks // quarter, slots, -1)
    chosen = jnp.transpose(chosen, (2, 0, 1, 3)).reshape(slots * quarter, full_width)
    window = lax.all_gather(chosen, IMG, axis=0, tiled=True)

    cross_keys = jnp.dot(window, x_key, preferred_element_type=jnp.float32).astype(jnp.bfloat16)
    cross_values = jnp.dot(window, x_value, preferred_element_type=jnp.float32).astype(jnp.bfloat16)
    start_row = shard_index * tokens
    positions = start_row + jnp.arange(tokens, dtype=jnp.int32)
    token_rank = jnp.sum((image_pos[None, :] <= positions[:, None]).astype(jnp.int32), axis=1) - 1
    first_image = jnp.sum((image_pos < start_row).astype(jnp.int32))
    local_slot = token_rank - first_image + 1
    key_slot = jnp.arange(slots * latent_rows, dtype=jnp.int32) // quarter % slots
    cross_visible = (key_slot[None, :] == local_slot[:, None])[None]
    cross_rows = cross_query.reshape(tokens, local_heads, HD)
    cross_scores = jnp.einsum(
        "thd,khd->htk",
        cross_rows,
        cross_keys.reshape(-1, local_heads, HD),
        preferred_element_type=jnp.float32,
    ) * HD ** (-0.5)
    cross_context = attend(cross_scores, cross_visible, cross_values.reshape(-1, local_heads, HD))
    cross_context = cross_context * jnp.tanh(cross_gate).reshape(local_heads, HD)
    cross_out = (
        jnp.where((token_rank >= 0)[:, None, None], cross_context, 0.0)
        .reshape(tokens, -1)
        .astype(jnp.bfloat16)
    )

    self_rows = self_attention(own_y.astype(jnp.int32)[None], head_query, pairs)
    self_rows = lax.all_to_all(self_rows, BLK, 0, 0, tiled=True)
    self_out = jnp.transpose(self_rows.reshape(y_size, z_size, piece, HD), (0, 2, 1, 3))
    return (cross_out, self_out.reshape(tokens, -1))


def solution(mesh):
    blocks, heads_of, documents = mesh.devices.shape
    z_size = 8
    devices = mesh.devices.reshape(blocks // z_size, z_size, 2, heads_of // 2, documents)
    inner = Mesh(devices, ("y", "z", "xl", "core", "doc"))
    rows = ("doc", "y", "z")
    in_specs = (
        P(rows, None, None),
        P(),
        P(),
        P(),
        P(),
        P(BLK, IMG),
        P(BLK, IMG),
        P(BLK, IMG),
        P(IMG, BLK),
        P(None, IMG),
        P(None, IMG),
        P(rows, IMG),
        P(rows, IMG),
        P(rows, IMG),
        P(rows, IMG),
        P(IMG),
        P("doc"),
    )
    out_specs = (P(rows, IMG), P(rows, IMG))
    return jax.shard_map(
        shards, mesh=inner, in_specs=in_specs, out_specs=out_specs, check_vma=False
    )
```

```python
import functools

import jax
import jax.numpy as jnp
from jax import lax
from jax.experimental import pallas as pl
from jax.experimental.pallas import tpu as pltpu
from jax.sharding import Mesh
from jax.sharding import PartitionSpec as P

HD = 128
RHD = 96
CITE = 3
BLK = ("y", "z")
IMG = ("xl", "core")
LOG2E = 1.4426950408889634
MIB = 1024 * 1024

epsilon = 1e-05

VMEM = pl.BlockSpec(memory_space=pltpu.VMEM)
SMEM = pl.BlockSpec(memory_space=pltpu.SMEM)


def layer_norm(values, gain):
    values = values.astype(jnp.float32)
    center = jnp.mean(values, -1, keepdims=True)
    spread = jnp.mean(jnp.square(values - center), -1, keepdims=True)
    return (values - center) * lax.rsqrt(spread + epsilon) * gain


def dot_t(left, right):
    return lax.dot_general(
        left, right, (((1,), (1,)), ((), ())), preferred_element_type=jnp.float32
    )


def call(kernel, out_shape, in_specs, name, flops, limit=40, scratch=()):
    return pl.pallas_call(
        kernel,
        out_shape=out_shape,
        in_specs=in_specs,
        out_specs=jax.tree.map(lambda _: VMEM, out_shape),
        scratch_shapes=list(scratch),
        compiler_params=pltpu.CompilerParams(vmem_limit_bytes=limit * MIB),
        cost_estimate=pl.CostEstimate(flops=flops, bytes_accessed=3000000, transcendentals=0),
        name=name,
    )


def pack_kernel(query_ref, key_ref, value_ref, out_ref, packed_ref):
    heads = query_ref.shape[1] // RHD
    copies = packed_ref.shape[0] // heads
    out_columns = out_ref[...].T
    for head in range(heads):
        span = slice(head * RHD, (head + 1) * RHD)
        row = jnp.concatenate(
            [query_ref[:, span], key_ref[:, span], value_ref[:, span], out_columns[:, span]], 1
        )
        for copy in range(copies):
            packed_ref[head * copies + copy] = row


def heads_kernel(core_ref, own_ref, other_ref, latent_ref, weight_ref, out_ref):
    core = core_ref[0]
    images, latent_rows, _ = out_ref.shape
    half = own_ref.shape[0] // images
    overlap = 2 * half - 257
    weight = weight_ref[...]

    def project(rows):
        return jnp.dot(rows, weight, preferred_element_type=jnp.float32).astype(jnp.bfloat16)

    latent = project(latent_ref[...])
    query = latent[:, :RHD]
    latent_key, latent_value = latent[:, RHD : 2 * RHD], latent[:, 2 * RHD : 3 * RHD]
    scale = RHD ** (-0.5)
    latent_scores = dot_t(query, latent_key) * scale
    latent_peak = jnp.max(latent_scores, -1, keepdims=True)
    place = lax.broadcasted_iota(jnp.int32, (latent_rows, half), 1)
    own_seen = place >= overlap * core
    other_seen = place >= overlap * (1 - core)
    own = jnp.dot(own_ref[...], weight, preferred_element_type=jnp.float32)
    other = jnp.dot(other_ref[...], weight, preferred_element_type=jnp.float32)
    for image in range(images):
        peak, parts = latent_peak, [(latent_scores, latent_value)]
        for rows, seen in ((own, own_seen), (other, other_seen)):
            rows = rows[image * half : (image + 1) * half].astype(jnp.bfloat16)
            scores = dot_t(query, rows[:, RHD : 2 * RHD]) * scale
            scores = jnp.where(seen, scores, -1e30)
            peak = jnp.maximum(peak, jnp.max(scores, -1, keepdims=True))
            parts.append((scores, rows[:, 2 * RHD : 3 * RHD]))
        total, context = 0.0, 0.0
        for scores, values in parts:
            weights = jnp.exp(scores - peak)
            total = total + jnp.sum(weights, -1, keepdims=True)
            context = context + jnp.dot(
                weights.astype(jnp.bfloat16), values, preferred_element_type=jnp.float32
            )
        out_ref[image] = (context / total).astype(jnp.bfloat16)


def project_kernel(*refs):
    parts, partial_ref = refs[:-1], refs[-1]
    count = len(parts) // 2
    total = 0.0
    for context_ref, weight_ref in zip(parts[:count], parts[count:]):
        total = total + dot_t(context_ref[...], weight_ref[...])
    partial_ref[...] = total


def cross_kernel(window_ref, key_ref, value_ref, query_ref, gate_ref, slot_ref, out_ref):
    stacks, flat, lanes = window_ref.shape
    quarter = 16
    tokens, columns = query_ref.shape
    count = stacks * quarter
    window = window_ref[...].reshape(stacks, flat // quarter, quarter, lanes)
    window = jnp.concatenate(
        [window[:, tile].reshape(count, lanes) for tile in range(flat // quarter)], 1
    )
    place = lax.broadcasted_iota(jnp.int32, (tokens, count), 1) // quarter % (CITE + 1)
    seen = place == slot_ref[...]
    scale = HD ** (-0.5)
    wide = 4 * HD
    for first in range(0, columns, wide):
        span = slice(first, first + wide)
        keys = jnp.dot(window, key_ref[:, span], preferred_element_type=jnp.float32)
        values = jnp.dot(window, value_ref[:, span], preferred_element_type=jnp.float32)
        keys, values = keys.astype(jnp.bfloat16), values.astype(jnp.bfloat16)
        for head in range(0, wide, HD):
            here = slice(head, head + HD)
            there = slice(first + head, first + head + HD)
            scores = dot_t(query_ref[:, there], keys[:, here]) * scale
            scores = jnp.where(seen, scores, -1e30)
            weights = jnp.exp(scores - jnp.max(scores, -1, keepdims=True))
            weights = jnp.where(seen, weights, 0.0)
            total = jnp.sum(weights, -1, keepdims=True)
            context = jnp.dot(
                weights.astype(jnp.bfloat16), values[:, here], preferred_element_type=jnp.float32
            )
            context = context / total * jnp.tanh(gate_ref[:, there])
            context = jnp.where(slot_ref[...] >= 0, context, 0.0)
            out_ref[:, there] = context.astype(jnp.bfloat16)


def self_kernel(own_ref, q_ref, kv_ref, o_ref, s_ref):
    own = own_ref[0]
    pieces, blocks, rows2, width = kv_ref.shape
    rows = rows2 // 2
    group = 128 // rows
    factor = width**-0.5 * LOG2E
    index_q = lax.broadcasted_iota(jnp.int32, (128, 128), 0)
    index_k = lax.broadcasted_iota(jnp.int32, (128, 128), 1)
    place_q = index_q // rows * 128 + own * rows + index_q % rows
    place_k = index_k // rows * 128 + index_k % rows
    for turn in range(blocks // group):
        first = turn * group
        query = q_ref[first : first + group].reshape(128, width)
        span = (first + group) * rows
        peak = None
        for piece in range(pieces):
            keys = kv_ref[piece, 0 : first + group, 0:rows, :].reshape(span, width)
            scores = lax.dot_general(
                query, keys, (((1,), (1,)), ((), ())), preferred_element_type=jnp.float32
            )
            scores = scores * factor
            tail = jnp.where(place_k + piece * rows <= place_q, scores[:, span - 128 :], -1e30)
            s_ref[piece, :, span - 128 : span] = tail
            top = jnp.max(tail, -1, keepdims=True)
            if span > 128:
                s_ref[piece, :, 0 : span - 128] = scores[:, : span - 128]
                top = jnp.maximum(top, jnp.max(scores[:, : span - 128], -1, keepdims=True))
            peak = top if peak is None else jnp.maximum(peak, top)
        total = jnp.zeros((128, 1), jnp.float32)
        context = jnp.zeros((128, width), jnp.float32)
        for piece in range(pieces):
            weights = jnp.exp2(s_ref[piece, :, 0:span] - peak)
            total = total + jnp.sum(weights, -1, keepdims=True)
            values = kv_ref[piece, 0 : first + group, rows : 2 * rows, :].reshape(span, width)
            context = context + jnp.dot(
                weights.astype(jnp.bfloat16), values, preferred_element_type=jnp.float32
            )
        o_ref[first : first + group] = (
            (context / total).astype(jnp.bfloat16).reshape(group, rows, width)
        )


def by_head(rows, y_size, z_size):
    tokens = rows.shape[0]
    split = rows.reshape(y_size, tokens // y_size, z_size, HD)
    return jnp.transpose(split, (0, 2, 1, 3)).reshape(y_size * z_size, tokens // y_size, HD)


def shards(
    features,
    latents,
    context_gain,
    latent_gain,
    final_gain,
    rs_query,
    rs_key,
    rs_value,
    rs_out,
    x_key,
    x_value,
    text_query,
    text_key,
    text_value,
    cross_query,
    cross_gate,
    image_pos,
):
    y_size, z_size = lax.axis_size("y"), lax.axis_size("z")
    blocks = y_size * z_size
    heads_of = lax.axis_size(IMG)
    shard_index = lax.axis_index(BLK)
    own_y = lax.axis_index("y").astype(jnp.int32)
    own_core = lax.axis_index("core").astype(jnp.int32)
    own_img = lax.axis_index(IMG)
    tokens = text_query.shape[0]
    piece = tokens // y_size
    latent_rows, full_width = latents.shape
    bf16, f32 = jnp.bfloat16, jnp.float32

    depth, columns = rs_query.shape
    weights = call(
        pack_kernel,
        jax.ShapeDtypeStruct((blocks, depth, 4 * RHD), bf16),
        [VMEM] * 4,
        "pack_weights",
        1000000,
    )(rs_query, rs_key, rs_value, rs_out)
    weights = lax.all_to_all(weights, BLK, 0, 0, tiled=True)
    weights = weights.reshape(blocks * depth, 4 * RHD)

    patches = features.shape[1]
    half = -(-patches // 16) * 8
    own_rows = lax.dynamic_slice_in_dim(features[0], own_core * (patches - half), half, 0)
    own_rows = layer_norm(own_rows, context_gain).astype(bf16)
    own_rows = lax.all_gather(own_rows, "y", axis=0, tiled=True)
    other_rows = lax.ppermute(own_rows, "core", [(0, 1), (1, 0)])
    latent_norm = layer_norm(latents, latent_gain).astype(bf16)

    packed = jnp.concatenate(
        [by_head(part, y_size, z_size) for part in (text_query, text_key, text_value)], 1
    )
    packed, weights = lax.optimization_barrier((packed, weights))
    packed = lax.all_to_all(packed, BLK, 0, 0, tiled=True)
    head_query = packed[:, 0:piece]
    pairs = lax.all_gather(packed[:, piece:], "y", axis=0, tiled=False)

    contexts = call(
        heads_kernel,
        jax.ShapeDtypeStruct((y_size, latent_rows, RHD), bf16),
        [SMEM] + [VMEM] * 4,
        "resampler_heads",
        1000000000,
    )(own_core[None], own_rows, other_rows, latent_norm, weights)

    out_weight = weights[:, 3 * RHD :]
    context_parts, weight_parts = [], []
    for step in range(y_size):
        part = lax.dynamic_index_in_dim(contexts, (own_y + step) % y_size, 0, keepdims=False)
        turn = [(source, (source + step) % y_size) for source in range(y_size)]
        context_parts.append(lax.ppermute(part, "y", turn) if step else part)
        weight_parts.append(lax.ppermute(out_weight, "y", turn) if step else out_weight)
    partial_out = call(
        project_kernel,
        jax.ShapeDtypeStruct((latent_rows, full_width), f32),
        [VMEM] * (2 * y_size),
        "project_out",
        70000000,
    )(*context_parts, *weight_parts)

    quarter = latent_rows // heads_of
    summed = lax.dynamic_slice_in_dim(partial_out, own_img * quarter, quarter, 0)
    for step in range(1, heads_of):
        part = lax.dynamic_slice_in_dim(partial_out, (own_img ^ step) * quarter, quarter, 0)
        pairs_of = [(source, source ^ step) for source in range(heads_of)]
        summed = summed + lax.ppermute(part, IMG, pairs_of)
    own_latents = lax.dynamic_slice_in_dim(latents, own_img * quarter, quarter, 0)
    resampled = layer_norm(own_latents.astype(f32) + summed, final_gain).astype(bf16)

    starts = jnp.arange(blocks, dtype=jnp.int32) * tokens
    image_rank = jnp.sum((image_pos[None, :] < image_pos[:, None]).astype(jnp.int32), axis=1)
    first_all = jnp.sum((image_pos[None, :] < starts[:, None]).astype(jnp.int32), axis=1)
    wanted = first_all[:, None] - 1 + jnp.arange(CITE + 1, dtype=jnp.int32)
    choice = (image_rank[None, None, :] == wanted[:, :, None]).astype(bf16)

    slots = CITE + 1
    tiles = full_width // 128
    chunk = quarter * tiles // blocks
    spread = jnp.transpose(resampled.reshape(quarter, tiles, 128), (1, 0, 2))
    spread = lax.all_to_all(spread.reshape(blocks, chunk, 128), BLK, 0, 0, tiled=True)
    chosen = jnp.einsum("dsi,icl->dscl", choice, spread, preferred_element_type=f32)
    chosen = chosen.astype(bf16).reshape(blocks, slots * chunk, 128)
    chosen = lax.all_to_all(chosen, BLK, 0, 0, tiled=True)
    chosen, pairs = lax.optimization_barrier((chosen, pairs))
    chosen = jnp.transpose(chosen.reshape(blocks, slots, chunk, 128), (1, 0, 2, 3))
    chosen = chosen.reshape(slots, blocks * chunk, 128)
    window = lax.all_gather(chosen, IMG, axis=0, tiled=True)

    start_row = shard_index * tokens
    positions = start_row + jnp.arange(tokens, dtype=jnp.int32)
    token_rank = jnp.sum((image_pos[None, :] <= positions[:, None]).astype(jnp.int32), axis=1) - 1
    first_image = jnp.sum((image_pos < start_row).astype(jnp.int32))
    local_slot = jnp.where(token_rank >= 0, token_rank - first_image + 1, -1)
    cross_out = call(
        cross_kernel,
        jax.ShapeDtypeStruct(cross_query.shape, bf16),
        [VMEM] * 6,
        "cross_attention",
        1500000000,
    )(window, x_key, x_value, cross_query, cross_gate[None], local_slot[:, None])

    self_rows = call(
        self_kernel,
        jax.ShapeDtypeStruct((blocks, piece, HD), bf16),
        [SMEM, VMEM, VMEM],
        "self_attention",
        1200000000,
        scratch=[pltpu.VMEM((y_size, 128, blocks * piece), f32)],
    )(own_y[None], head_query, pairs)
    self_rows = lax.all_to_all(self_rows, BLK, 0, 0, tiled=True)
    self_out = jnp.transpose(self_rows.reshape(y_size, z_size, piece, HD), (0, 2, 1, 3))
    return (cross_out, self_out.reshape(tokens, -1))


def solution(mesh):
    blocks, heads_of, documents = mesh.devices.shape
    z_size = 8
    devices = mesh.devices.reshape(blocks // z_size, z_size, 2, heads_of // 2, documents)
    inner = Mesh(devices, ("y", "z", "xl", "core", "doc"))
    rows = ("doc", "y", "z")
    in_specs = (
        P(rows, None, None),
        P(),
        P(),
        P(),
        P(),
        P(BLK, IMG),
        P(BLK, IMG),
        P(BLK, IMG),
        P(IMG, BLK),
        P(None, IMG),
        P(None, IMG),
        P(rows, IMG),
        P(rows, IMG),
        P(rows, IMG),
        P(rows, IMG),
        P(IMG),
        P("doc"),
    )
    out_specs = (P(rows, IMG), P(rows, IMG))
    return jax.shard_map(
        shards, mesh=inner, in_specs=in_specs, out_specs=out_specs, check_vma=False
    )
```

```python
import functools

import jax
import jax.numpy as jnp
from jax import lax
from jax.experimental import pallas as pl
from jax.experimental.pallas import tpu as pltpu
from jax.sharding import Mesh
from jax.sharding import PartitionSpec as P

HD = 128
RHD = 96
CITE = 3
BLK = ("y", "z")
IMG = ("xl", "core")
LOG2E = 1.4426950408889634
MIB = 1024 * 1024

epsilon = 1e-05

VMEM = pl.BlockSpec(memory_space=pltpu.VMEM)
SMEM = pl.BlockSpec(memory_space=pltpu.SMEM)


def layer_norm(values, gain):
    values = values.astype(jnp.float32)
    center = jnp.mean(values, -1, keepdims=True)
    spread = jnp.mean(jnp.square(values - center), -1, keepdims=True)
    return (values - center) * lax.rsqrt(spread + epsilon) * gain


def dot_t(left, right):
    return lax.dot_general(
        left, right, (((1,), (1,)), ((), ())), preferred_element_type=jnp.float32
    )


def call(kernel, out_shape, in_specs, name, flops, limit=40, scratch=()):
    return pl.pallas_call(
        kernel,
        out_shape=out_shape,
        in_specs=in_specs,
        out_specs=jax.tree.map(lambda _: VMEM, out_shape),
        scratch_shapes=list(scratch),
        compiler_params=pltpu.CompilerParams(vmem_limit_bytes=limit * MIB),
        cost_estimate=pl.CostEstimate(flops=flops, bytes_accessed=3000000, transcendentals=0),
        name=name,
    )


def pack_kernel(query_ref, key_ref, value_ref, out_ref, pair_key_ref, pair_value_ref, packed_ref):
    heads = query_ref.shape[1] // RHD
    copies = packed_ref.shape[0] // heads
    piece = pair_key_ref.shape[0] // heads
    out_columns = out_ref[...].T
    for head in range(heads):
        span = slice(head * RHD, (head + 1) * RHD)
        row = jnp.concatenate(
            [query_ref[:, span], key_ref[:, span], value_ref[:, span], out_columns[:, span]], 1
        ).astype(jnp.float32)
        row = jnp.concatenate([row[:, lane : lane + 128] for lane in range(0, 4 * RHD, 128)], 0)
        row = row.astype(jnp.bfloat16)
        here = slice(head * piece, (head + 1) * piece)
        for copy in range(copies):
            target = head * copies + copy
            lanes = slice(copy * HD, (copy + 1) * HD)
            packed_ref[target, 0:piece] = pair_key_ref[here, lanes]
            packed_ref[target, piece : 2 * piece] = pair_value_ref[here, lanes]
            packed_ref[target, 2 * piece :] = row


def heads_kernel(core_ref, own_ref, other_ref, latent_ref, weight_ref, out_ref):
    core = core_ref[0]
    images, latent_rows, _ = out_ref.shape
    half = own_ref.shape[0] // images
    overlap = 2 * half - 257
    packed = weight_ref[:, 64:, :].astype(jnp.float32)
    blocks, depth = packed.shape[0], packed.shape[1] // 3
    weight = jnp.concatenate(
        [packed[:, lane * depth : (lane + 1) * depth].reshape(blocks * depth, 128) for lane in range(3)],
        1,
    ).astype(jnp.bfloat16)

    def project(rows):
        return jnp.dot(rows, weight, preferred_element_type=jnp.float32).astype(jnp.bfloat16)

    latent = project(latent_ref[...])
    query = latent[:, :RHD]
    latent_key, latent_value = latent[:, RHD : 2 * RHD], latent[:, 2 * RHD : 3 * RHD]
    scale = RHD ** (-0.5)
    latent_scores = dot_t(query, latent_key) * scale
    latent_peak = jnp.max(latent_scores, -1, keepdims=True)
    place = lax.broadcasted_iota(jnp.int32, (latent_rows, half), 1)
    own_seen = place >= overlap * core
    other_seen = place >= overlap * (1 - core)
    own = jnp.dot(own_ref[...], weight, preferred_element_type=jnp.float32)
    other = jnp.dot(other_ref[...], weight, preferred_element_type=jnp.float32)
    for image in range(images):
        peak, parts = latent_peak, [(latent_scores, latent_value)]
        for rows, seen in ((own, own_seen), (other, other_seen)):
            rows = rows[image * half : (image + 1) * half].astype(jnp.bfloat16)
            scores = dot_t(query, rows[:, RHD : 2 * RHD]) * scale
            scores = jnp.where(seen, scores, -1e30)
            peak = jnp.maximum(peak, jnp.max(scores, -1, keepdims=True))
            parts.append((scores, rows[:, 2 * RHD : 3 * RHD]))
        total, context = 0.0, 0.0
        for scores, values in parts:
            weights = jnp.exp(scores - peak)
            total = total + jnp.sum(weights, -1, keepdims=True)
            context = context + jnp.dot(
                weights.astype(jnp.bfloat16), values, preferred_element_type=jnp.float32
            )
        context = jnp.concatenate([jnp.zeros((latent_rows, 128 - RHD), jnp.float32), context / total], 1)
        out_ref[image] = context.astype(jnp.bfloat16)


def project_kernel(*refs):
    parts, partial_ref = refs[:-1], refs[-1]
    count = len(parts) // 2
    total = 0.0
    for context_ref, weight_ref in zip(parts[:count], parts[count:]):
        total = total + dot_t(context_ref[...], weight_ref[...])
    partial_ref[...] = total


def cross_kernel(window_ref, key_ref, value_ref, query_ref, gate_ref, slot_ref, out_ref):
    stacks, flat, lanes = window_ref.shape
    quarter = 16
    tokens, columns = query_ref.shape
    count = stacks * quarter
    window = window_ref[...].reshape(stacks, flat // quarter, quarter, lanes)
    window = jnp.concatenate(
        [window[:, tile].reshape(count, lanes) for tile in range(flat // quarter)], 1
    )
    place = lax.broadcasted_iota(jnp.int32, (tokens, count), 1) // quarter % (CITE + 1)
    seen = place == slot_ref[...]
    scale = HD ** (-0.5)
    wide = 4 * HD
    for first in range(0, columns, wide):
        span = slice(first, first + wide)
        keys = jnp.dot(window, key_ref[:, span], preferred_element_type=jnp.float32)
        values = jnp.dot(window, value_ref[:, span], preferred_element_type=jnp.float32)
        keys, values = keys.astype(jnp.bfloat16), values.astype(jnp.bfloat16)
        for head in range(0, wide, HD):
            here = slice(head, head + HD)
            there = slice(first + head, first + head + HD)
            scores = dot_t(query_ref[:, there], keys[:, here]) * scale
            scores = jnp.where(seen, scores, -1e30)
            weights = jnp.exp(scores - jnp.max(scores, -1, keepdims=True))
            weights = jnp.where(seen, weights, 0.0)
            total = jnp.sum(weights, -1, keepdims=True)
            context = jnp.dot(
                weights.astype(jnp.bfloat16), values[:, here], preferred_element_type=jnp.float32
            )
            context = context / total * jnp.tanh(gate_ref[:, there])
            context = jnp.where(slot_ref[...] >= 0, context, 0.0)
            out_ref[:, there] = context.astype(jnp.bfloat16)


def self_kernel(own_ref, q_ref, kv_ref, o_ref, s_ref):
    own = own_ref[0]
    pieces, blocks, rows2, width = kv_ref.shape
    rows = rows2 // 2
    group = 128 // rows
    factor = width**-0.5 * LOG2E
    index_q = lax.broadcasted_iota(jnp.int32, (128, 128), 0)
    index_k = lax.broadcasted_iota(jnp.int32, (128, 128), 1)
    place_q = index_q // rows * 128 + own * rows + index_q % rows
    place_k = index_k // rows * 128 + index_k % rows
    for turn in range(blocks // group):
        first = turn * group
        query = q_ref[first : first + group].reshape(128, width)
        span = (first + group) * rows
        peak = None
        for piece in range(pieces):
            keys = kv_ref[piece, 0 : first + group, 0:rows, :].reshape(span, width)
            scores = lax.dot_general(
                query, keys, (((1,), (1,)), ((), ())), preferred_element_type=jnp.float32
            )
            scores = scores * factor
            tail = jnp.where(place_k + piece * rows <= place_q, scores[:, span - 128 :], -1e30)
            s_ref[piece, :, span - 128 : span] = tail
            top = jnp.max(tail, -1, keepdims=True)
            if span > 128:
                s_ref[piece, :, 0 : span - 128] = scores[:, : span - 128]
                top = jnp.maximum(top, jnp.max(scores[:, : span - 128], -1, keepdims=True))
            peak = top if peak is None else jnp.maximum(peak, top)
        total = jnp.zeros((128, 1), jnp.float32)
        context = jnp.zeros((128, width), jnp.float32)
        for piece in range(pieces):
            weights = jnp.exp2(s_ref[piece, :, 0:span] - peak)
            total = total + jnp.sum(weights, -1, keepdims=True)
            values = kv_ref[piece, 0 : first + group, rows : 2 * rows, :].reshape(span, width)
            context = context + jnp.dot(
                weights.astype(jnp.bfloat16), values, preferred_element_type=jnp.float32
            )
        o_ref[first : first + group] = (
            (context / total).astype(jnp.bfloat16).reshape(group, rows, width)
        )


def by_head(rows, y_size, z_size):
    tokens = rows.shape[0]
    split = rows.reshape(y_size, tokens // y_size, z_size, HD)
    return jnp.transpose(split, (0, 2, 1, 3)).reshape(y_size * z_size, tokens // y_size, HD)


def shards(
    features,
    latents,
    context_gain,
    latent_gain,
    final_gain,
    rs_query,
    rs_key,
    rs_value,
    rs_out,
    x_key,
    x_value,
    text_query,
    text_key,
    text_value,
    cross_query,
    cross_gate,
    image_pos,
):
    y_size, z_size = lax.axis_size("y"), lax.axis_size("z")
    blocks = y_size * z_size
    heads_of = lax.axis_size(IMG)
    shard_index = lax.axis_index(BLK)
    own_y = lax.axis_index("y").astype(jnp.int32)
    own_core = lax.axis_index("core").astype(jnp.int32)
    own_img = lax.axis_index(IMG)
    tokens = text_query.shape[0]
    piece = tokens // y_size
    latent_rows, full_width = latents.shape
    bf16, f32 = jnp.bfloat16, jnp.float32

    patches = features.shape[1]
    half = -(-patches // 16) * 8
    own_rows = lax.dynamic_slice_in_dim(features[0], own_core * (patches - half), half, 0)
    own_rows = layer_norm(own_rows, context_gain).astype(bf16)
    own_rows, rs_query = lax.optimization_barrier((own_rows, rs_query))
    own_rows = lax.all_gather(own_rows, "y", axis=0, tiled=True)
    other_rows = lax.ppermute(own_rows, "core", [(0, 1), (1, 0)])
    latent_norm = layer_norm(latents, latent_gain).astype(bf16)

    depth = rs_query.shape[0]
    weight_rows = depth * 4 * RHD // 128
    packed = call(
        pack_kernel,
        jax.ShapeDtypeStruct((blocks, 2 * piece + weight_rows, 128), bf16),
        [VMEM] * 6,
        "pack_targets",
        1000000,
    )(rs_query, rs_key, rs_value, rs_out, text_key, text_value)
    packed = lax.all_to_all(packed, BLK, 0, 0, tiled=True)
    out_weight = packed[:, 2 * piece + weight_rows - depth :].reshape(blocks * depth, 128)
    pairs = packed[:, 0 : 2 * piece]

    contexts = call(
        heads_kernel,
        jax.ShapeDtypeStruct((y_size, latent_rows, 128), bf16),
        [SMEM] + [VMEM] * 4,
        "resampler_heads",
        1000000000,
    )(own_core[None], own_rows, other_rows, latent_norm, packed)

    context_parts, weight_parts = [], []
    for step in range(y_size):
        part = lax.dynamic_index_in_dim(contexts, (own_y + step) % y_size, 0, keepdims=False)
        turn = [(source, (source + step) % y_size) for source in range(y_size)]
        context_parts.append(lax.ppermute(part, "y", turn) if step else part)
        weight_parts.append(lax.ppermute(out_weight, "y", turn) if step else out_weight)
    partial_out = call(
        project_kernel,
        jax.ShapeDtypeStruct((latent_rows, full_width), f32),
        [VMEM] * (2 * y_size),
        "project_out",
        70000000,
    )(*context_parts, *weight_parts)

    pairs, partial_out = lax.optimization_barrier((pairs, partial_out))
    pairs = lax.all_gather(pairs, "y", axis=0, tiled=False)

    quarter = latent_rows // heads_of
    summed = lax.dynamic_slice_in_dim(partial_out, own_img * quarter, quarter, 0)
    for step in range(1, heads_of):
        part = lax.dynamic_slice_in_dim(partial_out, (own_img ^ step) * quarter, quarter, 0)
        pairs_of = [(source, source ^ step) for source in range(heads_of)]
        summed = summed + lax.ppermute(part, IMG, pairs_of)
    own_latents = lax.dynamic_slice_in_dim(latents, own_img * quarter, quarter, 0)
    resampled = layer_norm(own_latents.astype(f32) + summed, final_gain).astype(bf16)

    starts = jnp.arange(blocks, dtype=jnp.int32) * tokens
    image_rank = jnp.sum((image_pos[None, :] < image_pos[:, None]).astype(jnp.int32), axis=1)
    first_all = jnp.sum((image_pos[None, :] < starts[:, None]).astype(jnp.int32), axis=1)
    wanted = first_all[:, None] - 1 + jnp.arange(CITE + 1, dtype=jnp.int32)
    choice = (image_rank[None, None, :] == wanted[:, :, None]).astype(bf16)

    slots = CITE + 1
    tiles = full_width // 128
    chunk = quarter * tiles // blocks
    spread = jnp.transpose(resampled.reshape(quarter, tiles, 128), (1, 0, 2))
    spread = spread.reshape(blocks, chunk, 128)
    head_query = by_head(text_query, y_size, z_size)
    padding = jnp.zeros((blocks, -chunk % 8, 128), bf16)
    spread = jnp.concatenate([head_query, spread, padding], 1)
    spread = lax.all_to_all(spread, BLK, 0, 0, tiled=True)
    head_query, spread = spread[:, 0:piece], spread[:, piece : piece + chunk]
    chosen = jnp.einsum("dsi,icl->dscl", choice, spread, preferred_element_type=f32)
    chosen = chosen.astype(bf16).reshape(blocks, slots * chunk, 128)
    chosen, head_query = lax.optimization_barrier((chosen, head_query))
    chosen = lax.all_to_all(chosen, BLK, 0, 0, tiled=True)
    arrived = chosen
    chosen = jnp.transpose(chosen.reshape(blocks, slots, chunk, 128), (1, 0, 2, 3))
    chosen = chosen.reshape(slots, blocks * chunk, 128)
    window = lax.all_gather(chosen, IMG, axis=0, tiled=True)

    start_row = shard_index * tokens
    positions = start_row + jnp.arange(tokens, dtype=jnp.int32)
    token_rank = jnp.sum((image_pos[None, :] <= positions[:, None]).astype(jnp.int32), axis=1) - 1
    first_image = jnp.sum((image_pos < start_row).astype(jnp.int32))
    local_slot = jnp.where(token_rank >= 0, token_rank - first_image + 1, -1)
    cross_out = call(
        cross_kernel,
        jax.ShapeDtypeStruct(cross_query.shape, bf16),
        [VMEM] * 6,
        "cross_attention",
        1500000000,
    )(window, x_key, x_value, cross_query, cross_gate[None], local_slot[:, None])

    self_rows = call(
        self_kernel,
        jax.ShapeDtypeStruct((blocks, piece, HD), bf16),
        [SMEM, VMEM, VMEM],
        "self_attention",
        1200000000,
        scratch=[pltpu.VMEM((y_size, 128, blocks * piece), f32)],
    )(own_y[None], head_query, pairs)
    self_rows, arrived = lax.optimization_barrier((self_rows, arrived))
    self_rows = lax.all_to_all(self_rows, BLK, 0, 0, tiled=True)
    self_out = jnp.transpose(self_rows.reshape(y_size, z_size, piece, HD), (0, 2, 1, 3))
    return (cross_out, self_out.reshape(tokens, -1))


def solution(mesh):
    blocks, heads_of, documents = mesh.devices.shape
    z_size = 8
    devices = mesh.devices.reshape(blocks // z_size, z_size, 2, heads_of // 2, documents)
    inner = Mesh(devices, ("y", "z", "xl", "core", "doc"))
    rows = ("doc", "y", "z")
    in_specs = (
        P(rows, None, None),
        P(),
        P(),
        P(),
        P(),
        P(BLK, IMG),
        P(BLK, IMG),
        P(BLK, IMG),
        P(IMG, BLK),
        P(None, IMG),
        P(None, IMG),
        P(rows, IMG),
        P(rows, IMG),
        P(rows, IMG),
        P(rows, IMG),
        P(IMG),
        P("doc"),
    )
    out_specs = (P(rows, IMG), P(rows, IMG))
    return jax.shard_map(
        shards, mesh=inner, in_specs=in_specs, out_specs=out_specs, check_vma=False
    )
```

```python
import functools

import jax
import jax.numpy as jnp
from jax import lax
from jax.experimental import pallas as pl
from jax.experimental.pallas import tpu as pltpu
from jax.sharding import Mesh
from jax.sharding import PartitionSpec as P

HD = 128
RHD = 96
CITE = 3
BLK = ("y", "z")
IMG = ("xl", "core")
LOG2E = 1.4426950408889634
MIB = 1024 * 1024

epsilon = 1e-05

VMEM = pl.BlockSpec(memory_space=pltpu.VMEM)
SMEM = pl.BlockSpec(memory_space=pltpu.SMEM)


def layer_norm(values, gain):
    values = values.astype(jnp.float32)
    center = jnp.mean(values, -1, keepdims=True)
    spread = jnp.mean(jnp.square(values - center), -1, keepdims=True)
    return (values - center) * lax.rsqrt(spread + epsilon) * gain


def dot_t(left, right):
    return lax.dot_general(
        left, right, (((1,), (1,)), ((), ())), preferred_element_type=jnp.float32
    )


def call(kernel, out_shape, in_specs, name, flops, limit=40, scratch=()):
    return pl.pallas_call(
        kernel,
        out_shape=out_shape,
        in_specs=in_specs,
        out_specs=jax.tree.map(lambda _: VMEM, out_shape),
        scratch_shapes=list(scratch),
        compiler_params=pltpu.CompilerParams(vmem_limit_bytes=limit * MIB),
        cost_estimate=pl.CostEstimate(flops=flops, bytes_accessed=3000000, transcendentals=0),
        name=name,
    )


def prelude_kernel(core_ref, context_gain, latent_gain, *refs):
    count = 8
    sources, (own_ref, latent_ref, packed_ref) = refs[:count], refs[count : count + 3]
    held, done = refs[count + 3 : 2 * count + 3], refs[2 * count + 3]
    copies = [
        pltpu.make_async_copy(source, target, done.at[place])
        for place, (source, target) in enumerate(zip(sources, held))
    ]
    for copy in copies:
        copy.start()
    features, latents, query, key, value, out, text_key, text_value = held
    for copy in copies[:2]:
        copy.wait()
    half, patches = own_ref.shape[0], features.shape[0]
    rows = features[...].astype(jnp.float32)
    rows = jnp.where(core_ref[0] == 0, rows[:half], rows[patches - half :])
    own_ref[...] = layer_norm(rows, context_gain[...].reshape(1, -1)).astype(jnp.bfloat16)
    latent_ref[...] = layer_norm(latents[...], latent_gain[...].reshape(1, -1)).astype(jnp.bfloat16)
    for copy in copies[2:]:
        copy.wait()
    heads = query.shape[1] // RHD
    images = packed_ref.shape[0] // heads
    piece = text_key.shape[0] // heads
    for head in range(heads):
        span = slice(head * RHD, (head + 1) * RHD)
        row = jnp.concatenate(
            [query[:, span], key[:, span], value[:, span], out[:, span]], 1
        ).astype(jnp.float32)
        row = jnp.concatenate([row[:, lane : lane + 128] for lane in range(0, 4 * RHD, 128)], 0)
        row = row.astype(jnp.bfloat16)
        here = slice(head * piece, (head + 1) * piece)
        for image in range(images):
            target = head * images + image
            lanes = slice(image * HD, (image + 1) * HD)
            packed_ref[target, 0:piece] = text_key[here, lanes]
            packed_ref[target, piece : 2 * piece] = text_value[here, lanes]
            packed_ref[target, 2 * piece :] = row


def heads_kernel(core_ref, own_ref, other_ref, latent_ref, weight_ref, out_ref):
    core = core_ref[0]
    images, latent_rows, _ = out_ref.shape
    half = own_ref.shape[0] // images
    overlap = 2 * half - 257
    packed = weight_ref[:, 64:, :].astype(jnp.float32)
    blocks, depth = packed.shape[0], packed.shape[1] // 3
    weight = jnp.concatenate(
        [packed[:, lane * depth : (lane + 1) * depth].reshape(blocks * depth, 128) for lane in range(3)],
        1,
    ).astype(jnp.bfloat16)

    def project(rows):
        return jnp.dot(rows, weight, preferred_element_type=jnp.float32).astype(jnp.bfloat16)

    latent = project(latent_ref[...])
    query = latent[:, :RHD]
    latent_key, latent_value = latent[:, RHD : 2 * RHD], latent[:, 2 * RHD : 3 * RHD]
    scale = RHD ** (-0.5)
    latent_scores = dot_t(query, latent_key) * scale
    latent_peak = jnp.max(latent_scores, -1, keepdims=True)
    place = lax.broadcasted_iota(jnp.int32, (latent_rows, half), 1)
    own_seen = place >= overlap * core
    other_seen = place >= overlap * (1 - core)
    own = jnp.dot(own_ref[...], weight, preferred_element_type=jnp.float32)
    other = jnp.dot(other_ref[...], weight, preferred_element_type=jnp.float32)
    for image in range(images):
        peak, parts = latent_peak, [(latent_scores, latent_value)]
        for rows, seen in ((own, own_seen), (other, other_seen)):
            rows = rows[image * half : (image + 1) * half].astype(jnp.bfloat16)
            scores = dot_t(query, rows[:, RHD : 2 * RHD]) * scale
            scores = jnp.where(seen, scores, -1e30)
            peak = jnp.maximum(peak, jnp.max(scores, -1, keepdims=True))
            parts.append((scores, rows[:, 2 * RHD : 3 * RHD]))
        total, context = 0.0, 0.0
        for scores, values in parts:
            weights = jnp.exp(scores - peak)
            total = total + jnp.sum(weights, -1, keepdims=True)
            context = context + jnp.dot(
                weights.astype(jnp.bfloat16), values, preferred_element_type=jnp.float32
            )
        context = jnp.concatenate([jnp.zeros((latent_rows, 128 - RHD), jnp.float32), context / total], 1)
        out_ref[image] = context.astype(jnp.bfloat16)


def project_kernel(*refs):
    parts, partial_ref = refs[:-1], refs[-1]
    count = len(parts) // 2
    total = 0.0
    for context_ref, weight_ref in zip(parts[:count], parts[count:]):
        total = total + dot_t(context_ref[...], weight_ref[...])
    partial_ref[...] = total


def cross_kernel(window_ref, key_ref, value_ref, query_ref, gate_ref, slot_ref, out_ref):
    stacks, flat, lanes = window_ref.shape
    quarter = 16
    tokens, columns = query_ref.shape
    count = stacks * quarter
    window = window_ref[...].reshape(stacks, flat // quarter, quarter, lanes)
    window = jnp.concatenate(
        [window[:, tile].reshape(count, lanes) for tile in range(flat // quarter)], 1
    )
    place = lax.broadcasted_iota(jnp.int32, (tokens, count), 1) // quarter % (CITE + 1)
    seen = place == slot_ref[...]
    scale = HD ** (-0.5)
    wide = 4 * HD
    for first in range(0, columns, wide):
        span = slice(first, first + wide)
        keys = jnp.dot(window, key_ref[:, span], preferred_element_type=jnp.float32)
        values = jnp.dot(window, value_ref[:, span], preferred_element_type=jnp.float32)
        keys, values = keys.astype(jnp.bfloat16), values.astype(jnp.bfloat16)
        for head in range(0, wide, HD):
            here = slice(head, head + HD)
            there = slice(first + head, first + head + HD)
            scores = dot_t(query_ref[:, there], keys[:, here]) * scale
            scores = jnp.where(seen, scores, -1e30)
            weights = jnp.exp(scores - jnp.max(scores, -1, keepdims=True))
            weights = jnp.where(seen, weights, 0.0)
            total = jnp.sum(weights, -1, keepdims=True)
            context = jnp.dot(
                weights.astype(jnp.bfloat16), values[:, here], preferred_element_type=jnp.float32
            )
            context = context / total * jnp.tanh(gate_ref[:, there])
            context = jnp.where(slot_ref[...] >= 0, context, 0.0)
            out_ref[:, there] = context.astype(jnp.bfloat16)


def self_kernel(own_ref, q_ref, kv_ref, o_ref, s_ref):
    own = own_ref[0]
    pieces, blocks, rows2, width = kv_ref.shape
    rows = rows2 // 2
    group = 128 // rows
    factor = width**-0.5 * LOG2E
    index_q = lax.broadcasted_iota(jnp.int32, (128, 128), 0)
    index_k = lax.broadcasted_iota(jnp.int32, (128, 128), 1)
    place_q = index_q // rows * 128 + own * rows + index_q % rows
    place_k = index_k // rows * 128 + index_k % rows
    for turn in range(blocks // group):
        first = turn * group
        query = q_ref[first : first + group].reshape(128, width)
        span = (first + group) * rows
        peak = None
        for piece in range(pieces):
            keys = kv_ref[piece, 0 : first + group, 0:rows, :].reshape(span, width)
            scores = lax.dot_general(
                query, keys, (((1,), (1,)), ((), ())), preferred_element_type=jnp.float32
            )
            scores = scores * factor
            tail = jnp.where(place_k + piece * rows <= place_q, scores[:, span - 128 :], -1e30)
            s_ref[piece, :, span - 128 : span] = tail
            top = jnp.max(tail, -1, keepdims=True)
            if span > 128:
                s_ref[piece, :, 0 : span - 128] = scores[:, : span - 128]
                top = jnp.maximum(top, jnp.max(scores[:, : span - 128], -1, keepdims=True))
            peak = top if peak is None else jnp.maximum(peak, top)
        total = jnp.zeros((128, 1), jnp.float32)
        context = jnp.zeros((128, width), jnp.float32)
        for piece in range(pieces):
            weights = jnp.exp2(s_ref[piece, :, 0:span] - peak)
            total = total + jnp.sum(weights, -1, keepdims=True)
            values = kv_ref[piece, 0 : first + group, rows : 2 * rows, :].reshape(span, width)
            context = context + jnp.dot(
                weights.astype(jnp.bfloat16), values, preferred_element_type=jnp.float32
            )
        o_ref[first : first + group] = (
            (context / total).astype(jnp.bfloat16).reshape(group, rows, width)
        )


def by_head(rows, y_size, z_size):
    tokens = rows.shape[0]
    split = rows.reshape(y_size, tokens // y_size, z_size, HD)
    return jnp.transpose(split, (0, 2, 1, 3)).reshape(y_size * z_size, tokens // y_size, HD)


def shards(
    features,
    latents,
    context_gain,
    latent_gain,
    final_gain,
    rs_query,
    rs_key,
    rs_value,
    rs_out,
    x_key,
    x_value,
    text_query,
    text_key,
    text_value,
    cross_query,
    cross_gate,
    image_pos,
):
    y_size, z_size = lax.axis_size("y"), lax.axis_size("z")
    blocks = y_size * z_size
    heads_of = lax.axis_size(IMG)
    shard_index = lax.axis_index(BLK)
    own_y = lax.axis_index("y").astype(jnp.int32)
    own_core = lax.axis_index("core").astype(jnp.int32)
    own_img = lax.axis_index(IMG)
    tokens = text_query.shape[0]
    piece = tokens // y_size
    latent_rows, full_width = latents.shape
    bf16, f32 = jnp.bfloat16, jnp.float32

    patches = features.shape[1]
    half = -(-patches // 16) * 8
    depth = rs_query.shape[0]
    weight_rows = depth * 4 * RHD // 128
    operands = (
        features[0],
        latents,
        rs_query,
        rs_key,
        rs_value,
        jnp.transpose(rs_out),
        text_key,
        text_value,
    )
    own_rows, latent_norm, packed = call(
        prelude_kernel,
        (
            jax.ShapeDtypeStruct((half, full_width), bf16),
            jax.ShapeDtypeStruct(latents.shape, bf16),
            jax.ShapeDtypeStruct((blocks, 2 * piece + weight_rows, 128), bf16),
        ),
        [SMEM, VMEM, VMEM] + [pl.BlockSpec(memory_space=pl.ANY)] * len(operands),
        "norm_and_pack",
        1000000,
        limit=60,
        scratch=[pltpu.VMEM(part.shape, part.dtype) for part in operands]
        + [pltpu.SemaphoreType.DMA((len(operands),))],
    )(own_core[None], context_gain, latent_gain, *operands)
    own_rows = lax.all_gather(own_rows, "y", axis=0, tiled=True)
    other_rows = lax.ppermute(own_rows, "core", [(0, 1), (1, 0)])
    packed = lax.all_to_all(packed, BLK, 0, 0, tiled=True)
    out_weight = packed[:, 2 * piece + weight_rows - depth :].reshape(blocks * depth, 128)
    pairs = packed[:, 0 : 2 * piece]

    contexts = call(
        heads_kernel,
        jax.ShapeDtypeStruct((y_size, latent_rows, 128), bf16),
        [SMEM] + [VMEM] * 4,
        "resampler_heads",
        1000000000,
    )(own_core[None], own_rows, other_rows, latent_norm, packed)

    context_parts, weight_parts = [], []
    for step in range(y_size):
        part = lax.dynamic_index_in_dim(contexts, (own_y + step) % y_size, 0, keepdims=False)
        turn = [(source, (source + step) % y_size) for source in range(y_size)]
        context_parts.append(lax.ppermute(part, "y", turn) if step else part)
        weight_parts.append(lax.ppermute(out_weight, "y", turn) if step else out_weight)
    partial_out = call(
        project_kernel,
        jax.ShapeDtypeStruct((latent_rows, full_width), f32),
        [VMEM] * (2 * y_size),
        "project_out",
        70000000,
    )(*context_parts, *weight_parts)

    pairs, partial_out = lax.optimization_barrier((pairs, partial_out))
    pairs = lax.all_gather(pairs, "y", axis=0, tiled=False)

    quarter = latent_rows // heads_of
    summed = lax.dynamic_slice_in_dim(partial_out, own_img * quarter, quarter, 0)
    for step in range(1, heads_of):
        part = lax.dynamic_slice_in_dim(partial_out, (own_img ^ step) * quarter, quarter, 0)
        pairs_of = [(source, source ^ step) for source in range(heads_of)]
        summed = summed + lax.ppermute(part, IMG, pairs_of)
    own_latents = lax.dynamic_slice_in_dim(latents, own_img * quarter, quarter, 0)
    resampled = layer_norm(own_latents.astype(f32) + summed, final_gain).astype(bf16)

    starts = jnp.arange(blocks, dtype=jnp.int32) * tokens
    image_rank = jnp.sum((image_pos[None, :] < image_pos[:, None]).astype(jnp.int32), axis=1)
    first_all = jnp.sum((image_pos[None, :] < starts[:, None]).astype(jnp.int32), axis=1)
    wanted = first_all[:, None] - 1 + jnp.arange(CITE + 1, dtype=jnp.int32)
    choice = (image_rank[None, None, :] == wanted[:, :, None]).astype(bf16)

    slots = CITE + 1
    tiles = full_width // 128
    chunk = quarter * tiles // blocks
    spread = jnp.transpose(resampled.reshape(quarter, tiles, 128), (1, 0, 2))
    spread = spread.reshape(blocks, chunk, 128)
    head_query = by_head(text_query, y_size, z_size)
    padding = jnp.zeros((blocks, -chunk % 8, 128), bf16)
    spread = jnp.concatenate([head_query, spread, padding], 1)
    spread = lax.all_to_all(spread, BLK, 0, 0, tiled=True)
    head_query, spread = spread[:, 0:piece], spread[:, piece : piece + chunk]
    chosen = jnp.einsum("dsi,icl->dscl", choice, spread, preferred_element_type=f32)
    chosen = chosen.astype(bf16).reshape(blocks, slots * chunk, 128)
    chosen, head_query = lax.optimization_barrier((chosen, head_query))
    chosen = lax.all_to_all(chosen, BLK, 0, 0, tiled=True)
    arrived = chosen
    chosen = jnp.transpose(chosen.reshape(blocks, slots, chunk, 128), (1, 0, 2, 3))
    chosen = chosen.reshape(slots, blocks * chunk, 128)
    window = lax.all_gather(chosen, IMG, axis=0, tiled=True)

    start_row = shard_index * tokens
    positions = start_row + jnp.arange(tokens, dtype=jnp.int32)
    token_rank = jnp.sum((image_pos[None, :] <= positions[:, None]).astype(jnp.int32), axis=1) - 1
    first_image = jnp.sum((image_pos < start_row).astype(jnp.int32))
    local_slot = jnp.where(token_rank >= 0, token_rank - first_image + 1, -1)
    cross_out = call(
        cross_kernel,
        jax.ShapeDtypeStruct(cross_query.shape, bf16),
        [VMEM] * 6,
        "cross_attention",
        1500000000,
    )(window, x_key, x_value, cross_query, cross_gate[None], local_slot[:, None])

    self_rows = call(
        self_kernel,
        jax.ShapeDtypeStruct((blocks, piece, HD), bf16),
        [SMEM, VMEM, VMEM],
        "self_attention",
        1200000000,
        scratch=[pltpu.VMEM((y_size, 128, blocks * piece), f32)],
    )(own_y[None], head_query, pairs)
    self_rows, arrived = lax.optimization_barrier((self_rows, arrived))
    self_rows = lax.all_to_all(self_rows, BLK, 0, 0, tiled=True)
    self_out = jnp.transpose(self_rows.reshape(y_size, z_size, piece, HD), (0, 2, 1, 3))
    return (cross_out, self_out.reshape(tokens, -1))


def solution(mesh):
    blocks, heads_of, documents = mesh.devices.shape
    z_size = 8
    devices = mesh.devices.reshape(blocks // z_size, z_size, 2, heads_of // 2, documents)
    inner = Mesh(devices, ("y", "z", "xl", "core", "doc"))
    rows = ("doc", "y", "z")
    in_specs = (
        P(rows, None, None),
        P(),
        P(),
        P(),
        P(),
        P(BLK, IMG),
        P(BLK, IMG),
        P(BLK, IMG),
        P(IMG, BLK),
        P(None, IMG),
        P(None, IMG),
        P(rows, IMG),
        P(rows, IMG),
        P(rows, IMG),
        P(rows, IMG),
        P(IMG),
        P("doc"),
    )
    out_specs = (P(rows, IMG), P(rows, IMG))
    return jax.shard_map(
        shards, mesh=inner, in_specs=in_specs, out_specs=out_specs, check_vma=False
    )
```

```python
import functools

import jax
import jax.numpy as jnp
from jax import lax
from jax.experimental import pallas as pl
from jax.experimental.pallas import tpu as pltpu
from jax.sharding import Mesh
from jax.sharding import PartitionSpec as P

HD = 128
RHD = 96
CITE = 3
BLK = ("y", "z")
IMG = ("xl", "core")
LOG2E = 1.4426950408889634
MIB = 1024 * 1024

epsilon = 1e-05

VMEM = pl.BlockSpec(memory_space=pltpu.VMEM)
SMEM = pl.BlockSpec(memory_space=pltpu.SMEM)


def layer_norm(values, gain):
    values = values.astype(jnp.float32)
    center = jnp.mean(values, -1, keepdims=True)
    spread = jnp.mean(jnp.square(values - center), -1, keepdims=True)
    return (values - center) * lax.rsqrt(spread + epsilon) * gain


def dot_t(left, right):
    return lax.dot_general(
        left, right, (((1,), (1,)), ((), ())), preferred_element_type=jnp.float32
    )


def call(kernel, out_shape, in_specs, name, flops, limit=40, scratch=()):
    return pl.pallas_call(
        kernel,
        out_shape=out_shape,
        in_specs=in_specs,
        out_specs=jax.tree.map(lambda _: VMEM, out_shape),
        scratch_shapes=list(scratch),
        compiler_params=pltpu.CompilerParams(vmem_limit_bytes=limit * MIB),
        cost_estimate=pl.CostEstimate(flops=flops, bytes_accessed=3000000, transcendentals=0),
        name=name,
    )


def prelude_kernel(core_ref, context_gain, latent_gain, *refs):
    count = 8
    sources, (own_ref, latent_ref, packed_ref) = refs[:count], refs[count : count + 3]
    held, done = refs[count + 3 : 2 * count + 3], refs[2 * count + 3]
    copies = [
        pltpu.make_async_copy(source, target, done.at[place])
        for place, (source, target) in enumerate(zip(sources, held))
    ]
    for copy in copies:
        copy.start()
    features, latents, query, key, value, out, text_key, text_value = held
    for copy in copies[:2]:
        copy.wait()
    half, patches = own_ref.shape[0], features.shape[0]
    rows = features[...].astype(jnp.float32)
    rows = jnp.where(core_ref[0] == 0, rows[:half], rows[patches - half :])
    own_ref[...] = layer_norm(rows, context_gain[...].reshape(1, -1)).astype(jnp.bfloat16)
    latent_ref[...] = layer_norm(latents[...], latent_gain[...].reshape(1, -1)).astype(jnp.bfloat16)
    for copy in copies[2:]:
        copy.wait()
    heads = query.shape[1] // RHD
    images = packed_ref.shape[0] // heads
    piece = text_key.shape[0] // heads
    for head in range(heads):
        span = slice(head * RHD, (head + 1) * RHD)
        row = jnp.concatenate(
            [query[:, span], key[:, span], value[:, span], out[:, span]], 1
        ).astype(jnp.float32)
        starts = [(up, 3 * RHD + lane) for up in range(0, 40, 8) for lane in (0, 32, 64)]
        starts += [(up, 256) for up in range(0, 40, 8)]
        blocks = [row[up : up + 8, lane : lane + 32] for up, lane in starts]
        mixed = [jnp.concatenate(blocks[at : at + 4], 1) for at in range(0, 20, 4)]
        row = jnp.concatenate([row[:, :128], row[:, 128:256], *mixed], 0)
        row = row.astype(jnp.bfloat16)
        here = slice(head * piece, (head + 1) * piece)
        for image in range(images):
            target = head * images + image
            lanes = slice(image * HD, (image + 1) * HD)
            packed_ref[target, 0:piece] = text_key[here, lanes]
            packed_ref[target, piece : 2 * piece] = text_value[here, lanes]
            packed_ref[target, 2 * piece :] = row


def heads_kernel(core_ref, own_ref, other_ref, latent_ref, weight_ref, out_ref):
    core = core_ref[0]
    images, latent_rows, _ = out_ref.shape
    half = own_ref.shape[0] // images
    overlap = 2 * half - 257
    packed = weight_ref[:, 64:, :].astype(jnp.float32)
    blocks, depth = packed.shape[0], packed.shape[1] // 3
    mixed = packed[:, 2 * depth :]
    rest = [mixed[:, 24:32, 96:]] + [mixed[:, 32:, lane : lane + 32] for lane in (0, 32, 64, 96)]
    parts = [packed[:, :depth], packed[:, depth : 2 * depth], jnp.concatenate(rest, 1)]
    weight = jnp.concatenate(
        [part.reshape(blocks * depth, part.shape[2]) for part in parts], 1
    ).astype(jnp.bfloat16)

    def project(rows):
        return jnp.dot(rows, weight, preferred_element_type=jnp.float32).astype(jnp.bfloat16)

    latent = project(latent_ref[...])
    query = latent[:, :RHD]
    latent_key, latent_value = latent[:, RHD : 2 * RHD], latent[:, 2 * RHD : 3 * RHD]
    scale = RHD ** (-0.5)
    latent_scores = dot_t(query, latent_key) * scale
    latent_peak = jnp.max(latent_scores, -1, keepdims=True)
    place = lax.broadcasted_iota(jnp.int32, (latent_rows, half), 1)
    own_seen = place >= overlap * core
    other_seen = place >= overlap * (1 - core)
    own = jnp.dot(own_ref[...], weight, preferred_element_type=jnp.float32)
    other = jnp.dot(other_ref[...], weight, preferred_element_type=jnp.float32)
    for image in range(images):
        peak, parts = latent_peak, [(latent_scores, latent_value)]
        for rows, seen in ((own, own_seen), (other, other_seen)):
            rows = rows[image * half : (image + 1) * half].astype(jnp.bfloat16)
            scores = dot_t(query, rows[:, RHD : 2 * RHD]) * scale
            scores = jnp.where(seen, scores, -1e30)
            peak = jnp.maximum(peak, jnp.max(scores, -1, keepdims=True))
            parts.append((scores, rows[:, 2 * RHD : 3 * RHD]))
        total, context = 0.0, 0.0
        for scores, values in parts:
            weights = jnp.exp(scores - peak)
            total = total + jnp.sum(weights, -1, keepdims=True)
            context = context + jnp.dot(
                weights.astype(jnp.bfloat16), values, preferred_element_type=jnp.float32
            )
        context = jnp.concatenate([jnp.zeros((latent_rows, 128 - RHD), jnp.float32), context / total], 1)
        out_ref[image] = context.astype(jnp.bfloat16)


def unpack_kernel(*refs):
    count = len(refs) // 2
    for packed_ref, out_ref in zip(refs[:count], refs[count:]):
        packed = packed_ref[...].astype(jnp.float32).reshape(32, 32, 128)
        rows = []
        for up in range(5):
            places = [divmod(3 * up + lane, 4) for lane in range(3)]
            rows.append(
                jnp.concatenate(
                    [packed[:, 8 * g : 8 * g + 8, 32 * at : 32 * at + 32] for g, at in places], 2
                )
            )
        rows = jnp.concatenate(rows, 1).reshape(out_ref.shape)
        out_ref[...] = rows.astype(jnp.bfloat16)


def project_kernel(*refs):
    parts, partial_ref = refs[:-1], refs[-1]
    count = len(parts) // 2
    total = 0.0
    for context_ref, weight_ref in zip(parts[:count], parts[count:]):
        total = total + dot_t(context_ref[...][:, 128 - RHD :], weight_ref[...])
    partial_ref[...] = total


def cross_kernel(window_ref, key_ref, value_ref, query_ref, gate_ref, slot_ref, out_ref):
    stacks, flat, lanes = window_ref.shape
    quarter = 16
    tokens, columns = query_ref.shape
    count = stacks * quarter
    window = window_ref[...].reshape(stacks, flat // quarter, quarter, lanes)
    window = jnp.concatenate(
        [window[:, tile].reshape(count, lanes) for tile in range(flat // quarter)], 1
    )
    place = lax.broadcasted_iota(jnp.int32, (tokens, count), 1) // quarter % (CITE + 1)
    seen = place == slot_ref[...]
    scale = HD ** (-0.5)
    wide = 4 * HD
    for first in range(0, columns, wide):
        span = slice(first, first + wide)
        keys = jnp.dot(window, key_ref[:, span], preferred_element_type=jnp.float32)
        values = jnp.dot(window, value_ref[:, span], preferred_element_type=jnp.float32)
        keys, values = keys.astype(jnp.bfloat16), values.astype(jnp.bfloat16)
        for head in range(0, wide, HD):
            here = slice(head, head + HD)
            there = slice(first + head, first + head + HD)
            scores = dot_t(query_ref[:, there], keys[:, here]) * scale
            scores = jnp.where(seen, scores, -1e30)
            weights = jnp.exp(scores - jnp.max(scores, -1, keepdims=True))
            weights = jnp.where(seen, weights, 0.0)
            total = jnp.sum(weights, -1, keepdims=True)
            context = jnp.dot(
                weights.astype(jnp.bfloat16), values[:, here], preferred_element_type=jnp.float32
            )
            context = context / total * jnp.tanh(gate_ref[:, there])
            context = jnp.where(slot_ref[...] >= 0, context, 0.0)
            out_ref[:, there] = context.astype(jnp.bfloat16)


def self_kernel(own_ref, q_ref, kv_ref, o_ref, s_ref):
    own = own_ref[0]
    pieces, blocks, rows2, width = kv_ref.shape
    rows = rows2 // 2
    group = 128 // rows
    factor = width**-0.5 * LOG2E
    index_q = lax.broadcasted_iota(jnp.int32, (128, 128), 0)
    index_k = lax.broadcasted_iota(jnp.int32, (128, 128), 1)
    place_q = index_q // rows * 128 + own * rows + index_q % rows
    place_k = index_k // rows * 128 + index_k % rows
    for turn in range(blocks // group):
        first = turn * group
        query = q_ref[first : first + group].reshape(128, width)
        span = (first + group) * rows
        peak = None
        for piece in range(pieces):
            keys = kv_ref[piece, 0 : first + group, 0:rows, :].reshape(span, width)
            scores = lax.dot_general(
                query, keys, (((1,), (1,)), ((), ())), preferred_element_type=jnp.float32
            )
            scores = scores * factor
            tail = jnp.where(place_k + piece * rows <= place_q, scores[:, span - 128 :], -1e30)
            s_ref[piece, :, span - 128 : span] = tail
            top = jnp.max(tail, -1, keepdims=True)
            if span > 128:
                s_ref[piece, :, 0 : span - 128] = scores[:, : span - 128]
                top = jnp.maximum(top, jnp.max(scores[:, : span - 128], -1, keepdims=True))
            peak = top if peak is None else jnp.maximum(peak, top)
        total = jnp.zeros((128, 1), jnp.float32)
        context = jnp.zeros((128, width), jnp.float32)
        for piece in range(pieces):
            weights = jnp.exp2(s_ref[piece, :, 0:span] - peak)
            total = total + jnp.sum(weights, -1, keepdims=True)
            values = kv_ref[piece, 0 : first + group, rows : 2 * rows, :].reshape(span, width)
            context = context + jnp.dot(
                weights.astype(jnp.bfloat16), values, preferred_element_type=jnp.float32
            )
        o_ref[first : first + group] = (
            (context / total).astype(jnp.bfloat16).reshape(group, rows, width)
        )


def by_head(rows, y_size, z_size):
    tokens = rows.shape[0]
    split = rows.reshape(y_size, tokens // y_size, z_size, HD)
    return jnp.transpose(split, (0, 2, 1, 3)).reshape(y_size * z_size, tokens // y_size, HD)


def shards(
    features,
    latents,
    context_gain,
    latent_gain,
    final_gain,
    rs_query,
    rs_key,
    rs_value,
    rs_out,
    x_key,
    x_value,
    text_query,
    text_key,
    text_value,
    cross_query,
    cross_gate,
    image_pos,
):
    y_size, z_size = lax.axis_size("y"), lax.axis_size("z")
    blocks = y_size * z_size
    heads_of = lax.axis_size(IMG)
    shard_index = lax.axis_index(BLK)
    own_y = lax.axis_index("y").astype(jnp.int32)
    own_core = lax.axis_index("core").astype(jnp.int32)
    own_img = lax.axis_index(IMG)
    tokens = text_query.shape[0]
    piece = tokens // y_size
    latent_rows, full_width = latents.shape
    bf16, f32 = jnp.bfloat16, jnp.float32

    patches = features.shape[1]
    half = -(-patches // 16) * 8
    depth = rs_query.shape[0]
    weight_rows = depth * 4 * RHD // 128
    operands = (
        features[0],
        latents,
        rs_query,
        rs_key,
        rs_value,
        jnp.transpose(rs_out),
        text_key,
        text_value,
    )
    own_rows, latent_norm, packed = call(
        prelude_kernel,
        (
            jax.ShapeDtypeStruct((half, full_width), bf16),
            jax.ShapeDtypeStruct(latents.shape, bf16),
            jax.ShapeDtypeStruct((blocks, 2 * piece + weight_rows, 128), bf16),
        ),
        [SMEM, VMEM, VMEM] + [pl.BlockSpec(memory_space=pl.ANY)] * len(operands),
        "norm_and_pack",
        1000000,
        limit=60,
        scratch=[pltpu.VMEM(part.shape, part.dtype) for part in operands]
        + [pltpu.SemaphoreType.DMA((len(operands),))],
    )(own_core[None], context_gain, latent_gain, *operands)
    own_rows = lax.all_gather(own_rows, "y", axis=0, tiled=True)
    other_rows = lax.ppermute(own_rows, "core", [(0, 1), (1, 0)])
    packed = lax.all_to_all(packed, BLK, 0, 0, tiled=True)
    first = 2 * piece + weight_rows - depth
    out_weight = packed[:, first : first + 32].reshape(blocks * 32, 128)
    pairs = packed[:, 0 : 2 * piece]

    contexts = call(
        heads_kernel,
        jax.ShapeDtypeStruct((y_size, latent_rows, 128), bf16),
        [SMEM] + [VMEM] * 4,
        "resampler_heads",
        1000000000,
    )(own_core[None], own_rows, other_rows, latent_norm, packed)

    context_parts, weight_parts = [], []
    for step in range(y_size):
        part = lax.dynamic_index_in_dim(contexts, (own_y + step) % y_size, 0, keepdims=False)
        turn = [(source, (source + step) % y_size) for source in range(y_size)]
        context_parts.append(lax.ppermute(part, "y", turn) if step else part)
        weight_parts.append(lax.ppermute(out_weight, "y", turn) if step else out_weight)
    weight_parts = call(
        unpack_kernel,
        tuple(jax.ShapeDtypeStruct((full_width, RHD), bf16) for _ in range(y_size)),
        [VMEM] * y_size,
        "unpack_o",
        1000000,
    )(*weight_parts)
    partial_out = call(
        project_kernel,
        jax.ShapeDtypeStruct((latent_rows, full_width), f32),
        [VMEM] * (2 * y_size),
        "project_out",
        70000000,
    )(*context_parts, *weight_parts)

    pairs, partial_out = lax.optimization_barrier((pairs, partial_out))
    pairs = lax.all_gather(pairs, "y", axis=0, tiled=False)

    quarter = latent_rows // heads_of
    summed = lax.dynamic_slice_in_dim(partial_out, own_img * quarter, quarter, 0)
    for step in range(1, heads_of):
        part = lax.dynamic_slice_in_dim(partial_out, (own_img ^ step) * quarter, quarter, 0)
        pairs_of = [(source, source ^ step) for source in range(heads_of)]
        summed = summed + lax.ppermute(part, IMG, pairs_of)
    own_latents = lax.dynamic_slice_in_dim(latents, own_img * quarter, quarter, 0)
    resampled = layer_norm(own_latents.astype(f32) + summed, final_gain).astype(bf16)

    starts = jnp.arange(blocks, dtype=jnp.int32) * tokens
    image_rank = jnp.sum((image_pos[None, :] < image_pos[:, None]).astype(jnp.int32), axis=1)
    first_all = jnp.sum((image_pos[None, :] < starts[:, None]).astype(jnp.int32), axis=1)
    wanted = first_all[:, None] - 1 + jnp.arange(CITE + 1, dtype=jnp.int32)
    choice = (image_rank[None, None, :] == wanted[:, :, None]).astype(bf16)

    slots = CITE + 1
    tiles = full_width // 128
    chunk = quarter * tiles // blocks
    spread = jnp.transpose(resampled.reshape(quarter, tiles, 128), (1, 0, 2))
    spread = spread.reshape(blocks, chunk, 128)
    head_query = by_head(text_query, y_size, z_size)
    padding = jnp.zeros((blocks, -chunk % 8, 128), bf16)
    spread = jnp.concatenate([head_query, spread, padding], 1)
    spread = lax.all_to_all(spread, BLK, 0, 0, tiled=True)
    head_query, spread = spread[:, 0:piece], spread[:, piece : piece + chunk]
    chosen = jnp.einsum("dsi,icl->dscl", choice, spread, preferred_element_type=f32)
    chosen = chosen.astype(bf16).reshape(blocks, slots * chunk, 128)
    chosen, head_query = lax.optimization_barrier((chosen, head_query))
    chosen = lax.all_to_all(chosen, BLK, 0, 0, tiled=True)
    arrived = chosen
    chosen = jnp.transpose(chosen.reshape(blocks, slots, chunk, 128), (1, 0, 2, 3))
    chosen = chosen.reshape(slots, blocks * chunk, 128)
    window = lax.all_gather(chosen, IMG, axis=0, tiled=True)

    start_row = shard_index * tokens
    positions = start_row + jnp.arange(tokens, dtype=jnp.int32)
    token_rank = jnp.sum((image_pos[None, :] <= positions[:, None]).astype(jnp.int32), axis=1) - 1
    first_image = jnp.sum((image_pos < start_row).astype(jnp.int32))
    local_slot = jnp.where(token_rank >= 0, token_rank - first_image + 1, -1)
    cross_out = call(
        cross_kernel,
        jax.ShapeDtypeStruct(cross_query.shape, bf16),
        [VMEM] * 6,
        "cross_attention",
        1500000000,
    )(window, x_key, x_value, cross_query, cross_gate[None], local_slot[:, None])

    self_rows = call(
        self_kernel,
        jax.ShapeDtypeStruct((blocks, piece, HD), bf16),
        [SMEM, VMEM, VMEM],
        "self_attention",
        1200000000,
        scratch=[pltpu.VMEM((y_size, 128, blocks * piece), f32)],
    )(own_y[None], head_query, pairs)
    self_rows, arrived = lax.optimization_barrier((self_rows, arrived))
    self_rows = lax.all_to_all(self_rows, BLK, 0, 0, tiled=True)
    self_out = jnp.transpose(self_rows.reshape(y_size, z_size, piece, HD), (0, 2, 1, 3))
    return (cross_out, self_out.reshape(tokens, -1))


def solution(mesh):
    blocks, heads_of, documents = mesh.devices.shape
    z_size = 8
    devices = mesh.devices.reshape(blocks // z_size, z_size, 2, heads_of // 2, documents)
    inner = Mesh(devices, ("y", "z", "xl", "core", "doc"))
    rows = ("doc", "y", "z")
    in_specs = (
        P(rows, None, None),
        P(),
        P(),
        P(),
        P(),
        P(BLK, IMG),
        P(BLK, IMG),
        P(BLK, IMG),
        P(IMG, BLK),
        P(None, IMG),
        P(None, IMG),
        P(rows, IMG),
        P(rows, IMG),
        P(rows, IMG),
        P(rows, IMG),
        P(IMG),
        P("doc"),
    )
    out_specs = (P(rows, IMG), P(rows, IMG))
    return jax.shard_map(
        shards, mesh=inner, in_specs=in_specs, out_specs=out_specs, check_vma=False
    )
```
